32 devices in a mesh: inner: 8 (over y, x, core), outer: 4 (over z).
Axes of the slice: x: 2, y: 2, z: 4, core: 2. Of those that a mesh axis runs over, the one named last changes fastest.
Arguments:
- embedding: bfloat16 [98304, 4096], P(('inner', 'outer')), may hold values from -80 to 80
- test_matrix: bfloat16 [4096, 256], replicated, may hold values from -0.09375 to 0.09375
Outputs:
- projection: float32 [4096, 256], P(('inner', 'outer'))
The draws below stay inside these ranges and needn't reach their ends.
All inputs are finite; a program needn't handle non-finite values.
Results may differ from the reference program's by a relative error of at most 0.00035.
Values sent between devices are 32-bit elements; how exact they have to be, the bound alone decides.
A program may use at most 128 MiB of HBM per device.

```python
import jax
import jax.numpy as jnp
from jax import lax

D = 4096
K = 256
ROWS = 98304


def draw_embedding(key, part):
    key = jax.random.fold_in(key, 11)
    key_base, key_rows, key_cols = jax.random.split(key, 3)
    position = jnp.arange(ROWS, dtype=jnp.float32) / ROWS
    base = jax.random.truncated_normal(key_base, -5.0, 5.0, (ROWS, D), jnp.float32)
    spread = 10.0
    row_scale = jnp.power(3.0, position) * jnp.power(spread, jax.random.uniform(key_rows, (ROWS,), jnp.float32)) / 4.0
    col_scale = jnp.power(spread, jax.random.uniform(key_cols, (D,), jnp.float32)) * 2.0 / spread
    return (base * row_scale[:, None] * col_scale[None, :]).astype(jnp.bfloat16)


def centred(own_key, dims, width, reach, kind=jnp.bfloat16):
    result = jax.random.normal(own_key, dims, jnp.float32) * width
    return jnp.minimum(jnp.maximum(result, -reach), reach).astype(kind)


def setup_inputs(seed: int = 0) -> dict:
    keys = jax.random.split(jax.random.key(seed), 3)
    return {
        "embedding": draw_embedding(jax.random.fold_in(keys[2], 71), 0),
        "test_matrix": centred(keys[1], (D, K), D ** -0.5, 0.09375),
    }


def reference(embedding, test_matrix):
    sketch = jnp.dot(embedding.astype(jnp.float32), test_matrix.astype(jnp.float32), preferred_element_type=jnp.float32)
    gram = jnp.dot(sketch.T.astype(jnp.float32), sketch.astype(jnp.float32), precision=lax.Precision.HIGHEST, preferred_element_type=jnp.float32)
    lower = jnp.linalg.cholesky(gram)
    basis = lax.linalg.triangular_solve(lower, sketch, left_side=False, lower=True, transpose_a=True).astype(jnp.bfloat16)
    return lax.dot_general(embedding.astype(jnp.float32), basis.astype(jnp.float32), (((0,), (0,)), ((), ())), preferred_element_type=jnp.float32)
```

```python
import functools

import jax
import jax.numpy as jnp
from jax import lax
from jax.experimental import pallas as pl
from jax.experimental.pallas import tpu as pltpu
from jax.sharding import PartitionSpec as P

MESH = pl.DeviceIdType.MESH
HIGHEST = lax.Precision.HIGHEST
VMEM_LIMIT = 56 * 1024 * 1024


def dot(a, b, precision=None):
    return jnp.dot(a, b, precision=precision, preferred_element_type=jnp.float32)


def gram_kernel(
    n_in, n_out, steps, e_ref, t_ref, st_ref, g_ref,
    acc, whole, recv1, recv2, s1, r1, s2, r2, s3, r3,
):
    step = pl.program_id(0)
    me_in, me_out = lax.axis_index("inner"), lax.axis_index("outer")
    rows = acc.shape[0] // n_in
    barrier = pltpu.get_barrier_semaphore()
    in_peers = [lax.rem(me_in + d, n_in) for d in range(n_in)]
    out_peers = [lax.rem(me_out + d, n_out) for d in range(n_out)]

    @pl.when(step == 0)
    def _():
        for d in range(1, n_in):
            pl.semaphore_signal(barrier, inc=1, device_id=(in_peers[d], me_out), device_id_type=MESH)
        for d in range(1, n_out):
            pl.semaphore_signal(barrier, inc=1, device_id=(me_in, out_peers[d]), device_id_type=MESH)
        acc[...] = jnp.zeros_like(acc)

    s = dot(e_ref[...], t_ref[...])
    st = s.T
    st_ref[...] = st
    acc[...] += dot(st, s, HIGHEST)

    @pl.when(step == steps - 1)
    def _():
        pl.semaphore_wait(barrier, n_in + n_out - 2)
        copies = []
        for d in range(1, n_in):
            peer = in_peers[d]
            copies.append(pltpu.make_async_remote_copy(
                src_ref=acc.at[pl.ds(pl.multiple_of(peer * rows, rows), rows), :],
                dst_ref=recv1.at[d],
                send_sem=s1.at[d], recv_sem=r1.at[d],
                device_id=(peer, me_out), device_id_type=MESH,
            ))
            copies[-1].start()
        total = acc[pl.ds(pl.multiple_of(me_in * rows, rows), rows), :]
        for d in range(1, n_in):
            copies[d - 1].wait_recv()
            total += recv1[d]
        recv2[me_out] = total
        seconds = []
        for d in range(1, n_out):
            seconds.append(pltpu.make_async_remote_copy(
                src_ref=recv2.at[me_out],
                dst_ref=recv2.at[me_out],
                send_sem=s2.at[d], recv_sem=r2.at[d],
                device_id=(me_in, out_peers[d]), device_id_type=MESH,
            ))
            seconds[-1].start()
        for c in copies:
            c.wait_send()
        for c in seconds:
            c.wait_recv()
        total = recv2[0]
        for d in range(1, n_out):
            total += recv2[d]
        mine = pl.ds(pl.multiple_of(me_in * rows, rows), rows)
        whole[mine, :] = total
        thirds = []
        for d in range(1, n_in):
            thirds.append(pltpu.make_async_remote_copy(
                src_ref=whole.at[mine, :],
                dst_ref=whole.at[mine, :],
                send_sem=s3.at[d], recv_sem=r3.at[d],
                device_id=(in_peers[d], me_out), device_id_type=MESH,
            ))
            thirds[-1].start()
        for c in seconds:
            c.wait_send()
        for c in thirds:
            c.wait()
        g_ref[...] = whole[...]


def sketch_and_gram(embedding, test_matrix, n_in, n_out):
    rows, width = embedding.shape
    rank = test_matrix.shape[1]
    chunk = 256
    steps = rows // chunk
    part = rank // n_in
    dma = pltpu.SemaphoreType.DMA
    return pl.pallas_call(
        functools.partial(gram_kernel, n_in, n_out, steps),
        grid=(steps,),
        out_shape=(
            jax.ShapeDtypeStruct((rank, rows), jnp.float32),
            jax.ShapeDtypeStruct((rank, rank), jnp.float32),
        ),
        in_specs=[
            pl.BlockSpec((chunk, width), lambda i: (i, 0)),
            pl.BlockSpec((width, rank), lambda i: (0, 0)),
        ],
        out_specs=(
            pl.BlockSpec((rank, chunk), lambda i: (0, i)),
            pl.BlockSpec(memory_space=pltpu.VMEM),
        ),
        scratch_shapes=[
            pltpu.VMEM((rank, rank), jnp.float32),
            pltpu.VMEM((rank, rank), jnp.float32),
            pltpu.VMEM((n_in, part, rank), jnp.float32),
            pltpu.VMEM((n_out, part, rank), jnp.float32),
            dma((n_in,)), dma((n_in,)), dma((n_out,)), dma((n_out,)), dma((n_in,)), dma((n_in,)),
        ],
        compiler_params=pltpu.CompilerParams(
            collective_id=0, has_side_effects=True, vmem_limit_bytes=VMEM_LIMIT,
        ),
        cost_estimate=pl.CostEstimate(
            flops=2 * rows * width * rank, bytes_accessed=rows * width * 2, transcendentals=0
        ),
    )(embedding, test_matrix)


def sweep(src, dst):
    n = src.shape[0]
    groups = n // 8
    lane = lax.broadcasted_iota(jnp.int32, (8, n), 1)
    sub = lax.broadcasted_iota(jnp.int32, (8, n), 0)
    full = (8, n)
    t = [src[8 * i : 8 * i + 8, :] for i in range(groups)]
    for g in range(groups):
        base = 8 * g
        panel = (lane >= base) & (lane < base + 8)
        cols = [jnp.broadcast_to(t[g][:, base + k : base + k + 1], full) for k in range(8)]
        top = jnp.where(panel, 0.0, t[g])
        scaled, splats, pivots = [], [], None
        for k in range(8):
            pivot = jnp.broadcast_to(cols[k][k : k + 1, :], full)
            inv = 1.0 / pivot
            row = jnp.broadcast_to(top[k : k + 1, :], full)
            scaled.append(jnp.where(lane == base + k, inv, row * inv))
            splat = {l: jnp.broadcast_to(cols[l][k : k + 1, :], full) * inv for l in range(k + 1, 8)}
            splats.append(splat)
            pivots = pivot if k == 0 else jnp.where(sub >= k, pivot, pivots)
            if k < 7:
                below = jnp.where(sub > k, cols[k], 0.0)
                for l in range(k + 1, 8):
                    cols[l] = cols[l] - below * splat[l]
                top = top - below * scaled[k]
        rows = jnp.where(lane == base + sub, 1.0, jnp.where(lane < base + 8, top, 0.0))
        dst[base : base + 8, :] = rows / jnp.sqrt(pivots)
        for i in range(g + 1, groups):
            c = [jnp.broadcast_to(t[i][:, base + k : base + k + 1], full) for k in range(8)]
            x = jnp.where(panel, 0.0, t[i])
            for k in range(8):
                for l in range(k + 1, 8):
                    c[l] = c[l] - c[k] * splats[k][l]
                x = x - c[k] * scaled[k]
            t[i] = x


def factor_kernel(g_ref, m_ref, a, m, x):
    half = a.shape[0]
    step = pl.program_id(0)

    @pl.when(step == 0)
    def _():
        a[...] = g_ref[:half, :half]

    @pl.when(step == 1)
    def _():
        x[...] = dot(m[...], g_ref[:half, half:], HIGHEST)
        a[...] = g_ref[half:, half:] - dot(x[...].T, x[...], HIGHEST)

    @pl.when(step == 1)
    def _():
        m_ref[:half, :half] = m[...]
        m_ref[:half, half:] = jnp.zeros_like(m)

    sweep(a, m)

    @pl.when(step == 1)
    def _():
        m_ref[half:, half:] = m[...]
        y = dot(x[...].T, m_ref[:half, :half], HIGHEST)
        m_ref[half:, :half] = -dot(m[...], y, HIGHEST)


def inverse_factor(gram):
    n = gram.shape[0]
    half = n // 2
    block = pltpu.VMEM((half, half), jnp.float32)
    return pl.pallas_call(
        factor_kernel,
        grid=(2,),
        out_shape=jax.ShapeDtypeStruct((n, n), jnp.float32),
        in_specs=[pl.BlockSpec(memory_space=pltpu.VMEM)],
        out_specs=pl.BlockSpec(memory_space=pltpu.VMEM),
        scratch_shapes=[block, block, block],
    )(gram)


def project_kernel(
    n_in, n_out, m_ref, st_ref, e_ref, out_ref,
    ebuf, basis, part, recv1, *rest,
):
    bits = n_in.bit_length() - 1
    rounds = bits - 1
    recv_a, recv_b = rest[:rounds], rest[rounds : 2 * rounds]
    last, esem, s1, r1, sa, ra, sb, rb, sz, rz = rest[2 * rounds :]
    me_in, me_out = lax.axis_index("inner"), lax.axis_index("outer")
    width = ebuf.shape[2]
    rank = basis.shape[0]
    half = rank // 2

    def flipped(r):
        index = me_in
        for b in range(bits):
            if r >> b & 1:
                bit = lax.rem(me_in // (1 << b), 2)
                index = index + (1 - 2 * bit) * (1 << b)
        return index

    peers = [flipped(1 << b) for b in range(bits)]
    out_peers = [lax.rem(me_out + d, n_out) for d in range(n_out)]
    barrier = pltpu.get_barrier_semaphore()
    for p in peers:
        pl.semaphore_signal(barrier, inc=1, device_id=(p, me_out), device_id_type=MESH)
    for d in range(1, n_out):
        pl.semaphore_signal(barrier, inc=1, device_id=(me_in, out_peers[d]), device_id_type=MESH)

    order = sorted(range(n_in // 2), key=lambda r: (-bin(r).count("1"), r))
    sequence = [2 * r + 1 for r in order] + [2 * r for r in order]
    loads = {}
    for r in sequence:
        start = pl.multiple_of(flipped(r) * width, width)
        loads[r] = pltpu.make_async_copy(e_ref.at[:, pl.ds(start, width)], ebuf.at[r], esem.at[r])
        loads[r].start()

    rows = basis.shape[1]
    for c in range(0, rows, 512):
        basis[:, c : c + 512] = dot(m_ref[...], st_ref[:, c : c + 512], HIGHEST).astype(jnp.bfloat16)

    pl.semaphore_wait(barrier, bits + n_out - 1)

    def remote(src, dst, send, recv, device):
        copy = pltpu.make_async_remote_copy(
            src_ref=src, dst_ref=dst, send_sem=send, recv_sem=recv,
            device_id=device, device_id_type=MESH,
        )
        copy.start()
        return copy

    sent = []
    first = {}
    for r in order:
        loads[2 * r + 1].wait()
        part[r] = dot(basis[...], ebuf[2 * r + 1]).T
        first[r] = remote(part.at[r], recv1.at[r], s1.at[r], r1.at[r], (peers[0], me_out))
        sent.append(first[r])

    lanes = {"a": pl.ds(0, half), "b": pl.ds(half, half)}
    way = {"a": list(range(1, bits)), "b": list(range(bits - 1, 0, -1))}
    bufs = {"a": recv_a, "b": recv_b}
    sems = {"a": (sa, ra), "b": (sb, rb)}
    pending = {}
    count = {"a": 0, "b": 0}

    def squeeze(index, remaining, b):
        at = remaining.index(b)
        return (index >> (at + 1) << at) | (index & ((1 << at) - 1))

    def send_chunk(which, stage, index, src):
        remaining = sorted(way[which][stage:])
        b = way[which][stage]
        at = remaining.index(b)
        target = squeeze(index, remaining, b)
        if index >> at & 1:
            k = count[which]
            count[which] += 1
            send, recv = sems[which]
            pending[which, stage, target] = remote(
                src, bufs[which][stage].at[target], send.at[k], recv.at[k], (peers[b], me_out)
            )
            sent.append(pending[which, stage, target])

    for r in order:
        loads[2 * r].wait()
        own = dot(basis[...], ebuf[2 * r]).T
        first[r].wait_recv()
        recv1[r] = recv1[r] + own
        for which in ("a", "b"):
            send_chunk(which, 0, r, recv1.at[r, :, lanes[which]])

    for stage in range(rounds):
        for which in ("a", "b"):
            remaining = sorted(way[which][stage:])
            b = way[which][stage]
            at = remaining.index(b)
            slots = sorted(range(1 << (len(remaining) - 1)), key=lambda v: (-bin(v).count("1"), v))
            for target in slots:
                index = (target >> at << (at + 1)) | (target & ((1 << at) - 1))
                pending[which, stage, target].wait_recv()
                buf = bufs[which][stage]
                if stage == 0:
                    kept = recv1[index, :, lanes[which]]
                else:
                    kept = bufs[which][stage - 1][index]
                buf[target] = buf[target] + kept
                if stage + 1 < rounds:
                    send_chunk(which, stage + 1, target, buf.at[target])

    block = out_ref.shape[0]
    finals = []
    for d in range(1, n_out):
        theirs = pl.ds(pl.multiple_of(out_peers[d] * block, block), block)
        for w, which in enumerate(("a", "b")):
            finals.append(remote(
                bufs[which][-1].at[0, theirs, :], last.at[me_out, :, lanes[which]],
                sz.at[w, d], rz.at[w, d], (me_in, out_peers[d]),
            ))
    mine = pl.ds(pl.multiple_of(me_out * block, block), block)
    for which in ("a", "b"):
        last[me_out, :, lanes[which]] = bufs[which][-1][0, mine, :]
    for c in finals:
        c.wait_recv()
    total = last[0]
    for d in range(1, n_out):
        total = total + last[d]
    out_ref[...] = total
    for c in sent + finals:
        c.wait_send()


def project(inverse, sketch_t, embedding, n_in, n_out):
    rows, width = embedding.shape
    rank = inverse.shape[0]
    block = width // n_in
    bits = n_in.bit_length() - 1
    rounds = bits - 1
    dma = pltpu.SemaphoreType.DMA
    f32 = jnp.float32
    halves = [pltpu.VMEM((n_in >> (s + 2), block, rank // 2), f32) for s in range(rounds)]
    vmem = pl.BlockSpec(memory_space=pltpu.VMEM)
    return pl.pallas_call(
        functools.partial(project_kernel, n_in, n_out),
        out_shape=jax.ShapeDtypeStruct((block // n_out, rank), f32),
        in_specs=[vmem, vmem, pl.BlockSpec(memory_space=pl.ANY)],
        out_specs=vmem,
        scratch_shapes=[
            pltpu.VMEM((n_in, rows, block), jnp.bfloat16),
            pltpu.VMEM((rank, rows), jnp.bfloat16),
            pltpu.VMEM((n_in // 2, block, rank), f32),
            pltpu.VMEM((n_in // 2, block, rank), f32),
            *halves,
            *halves,
            pltpu.VMEM((n_out, block // n_out, rank), f32),
            dma((n_in,)),
            dma((n_in // 2,)), dma((n_in // 2,)),
            dma((n_in // 2,)), dma((n_in // 2,)),
            dma((n_in // 2,)), dma((n_in // 2,)),
            dma((2, n_out)), dma((2, n_out)),
        ],
        compiler_params=pltpu.CompilerParams(
            collective_id=1, has_side_effects=True, vmem_limit_bytes=VMEM_LIMIT,
        ),
        cost_estimate=pl.CostEstimate(
            flops=2 * rows * width * rank, bytes_accessed=rows * width * 2, transcendentals=0
        ),
    )(inverse, sketch_t, embedding)


def local(n_in, n_out, embedding, test_matrix):
    sketch_t, gram = sketch_and_gram(embedding, test_matrix, n_in, n_out)
    inverse = inverse_factor(gram)
    return project(inverse, sketch_t, embedding, n_in, n_out)


def solution(mesh):
    n_in, n_out = mesh.shape["inner"], mesh.shape["outer"]
    return jax.shard_map(
        functools.partial(local, n_in, n_out),
        mesh=mesh,
        in_specs=(P(("inner", "outer"), None), P()),
        out_specs=P(("inner", "outer"), None),
        check_vma=False,
    )
```

```python
import functools

import jax
import jax.numpy as jnp
from jax import lax
from jax.experimental import pallas as pl
from jax.experimental.pallas import tpu as pltpu
from jax.sharding import PartitionSpec as P

MESH = pl.DeviceIdType.MESH
HIGHEST = lax.Precision.HIGHEST
VMEM_LIMIT = 58 * 1024 * 1024
CHUNK = 384


def dot(a, b, precision=None):
    return jnp.dot(a, b, precision=precision, preferred_element_type=jnp.float32)


def remote(src, dst, send, recv, device):
    copy = pltpu.make_async_remote_copy(
        src_ref=src, dst_ref=dst, send_sem=send, recv_sem=recv,
        device_id=device, device_id_type=MESH,
    )
    copy.start()
    return copy


def sweep(a, store):
    n = a.shape[0]
    groups = n // 8
    lane = lax.broadcasted_iota(jnp.int32, (8, n), 1)
    sub = lax.broadcasted_iota(jnp.int32, (8, n), 0)
    full = (8, n)
    t = [a[8 * i : 8 * i + 8, :] for i in range(groups)]
    for g in range(groups):
        base = 8 * g
        panel = (lane >= base) & (lane < base + 8)
        cols = [jnp.broadcast_to(t[g][:, base + k : base + k + 1], full) for k in range(8)]
        top = jnp.where(panel, 0.0, t[g])
        scaled, splats, pivots = [], [], None
        for k in range(8):
            pivot = jnp.broadcast_to(cols[k][k : k + 1, :], full)
            inv = 1.0 / pivot
            row = jnp.broadcast_to(top[k : k + 1, :], full)
            scaled.append(jnp.where(lane == base + k, inv, row * inv))
            splat = {l: jnp.broadcast_to(cols[l][k : k + 1, :], full) * inv for l in range(k + 1, 8)}
            splats.append(splat)
            pivots = pivot if k == 0 else jnp.where(sub >= k, pivot, pivots)
            if k < 7:
                below = jnp.where(sub > k, cols[k], 0.0)
                for l in range(k + 1, 8):
                    cols[l] = cols[l] - below * splat[l]
                top = top - below * scaled[k]
        rows = jnp.where(lane == base + sub, 1.0, jnp.where(lane < base + 8, top, 0.0))
        store(base, rows / jnp.sqrt(pivots))
        for first in range(g + 1, groups, 4):
            those = range(first, min(first + 4, groups))
            old = jnp.stack([t[i] for i in those])
            c = [jnp.broadcast_to(old[:, :, base + k : base + k + 1], old.shape) for k in range(8)]
            x = jnp.where(panel, 0.0, old)
            for k in range(8):
                for l in range(k + 1, 8):
                    c[l] = c[l] - c[k] * splats[k][l]
                x = x - c[k] * scaled[k]
            for at, i in enumerate(those):
                t[i] = x[at]


def kernel(
    n_in, n_out, e_ref, t_ref, out_ref,
    ebuf, tbuf, s_last, st, basis, acc, whole, recv1, recv2, m,
    part, first, stages, final, last,
    esem, tsem, s1, r1, s2, r2, s3, r3, sc, rc, sw, rw, sz, rz,
):
    me_in, me_out = lax.axis_index("inner"), lax.axis_index("outer")
    rows, width = ebuf.shape
    rank = acc.shape[0]
    half = rank // 2
    bits = n_in.bit_length() - 1
    rounds = bits - 1
    block = width // n_in
    out_block = block // n_out
    steps = rows // CHUNK

    barrier = pltpu.get_barrier_semaphore()
    in_peers = [lax.rem(me_in + d, n_in) for d in range(n_in)]
    out_peers = [lax.rem(me_out + d, n_out) for d in range(n_out)]
    for d in range(1, n_in):
        pl.semaphore_signal(barrier, inc=1, device_id=(in_peers[d], me_out), device_id_type=MESH)
    for d in range(1, n_out):
        pl.semaphore_signal(barrier, inc=1, device_id=(me_in, out_peers[d]), device_id_type=MESH)

    test_copy = pltpu.make_async_copy(t_ref, tbuf, tsem)
    test_copy.start()

    def load(i):
        span = pl.ds(pl.multiple_of(i * CHUNK, CHUNK), CHUNK)
        return pltpu.make_async_copy(e_ref.at[span, :], ebuf.at[span, :], esem.at[i])

    for i in range(steps):
        load(i).start()

    def sketch(i):
        span = pl.ds(pl.multiple_of(i * CHUNK, CHUNK), CHUNK)
        return dot(ebuf[span, :], tbuf[...])

    def keep(i, s):
        span = pl.ds(pl.multiple_of(i * CHUNK, CHUNK), CHUNK)
        s_last[...] = s
        st[:, span] = s.T

    def gram_term(i):
        span = pl.ds(pl.multiple_of(i * CHUNK, CHUNK), CHUNK)
        return dot(st[:, span], s_last[...], HIGHEST)

    test_copy.wait()
    load(0).wait()
    keep(0, sketch(0))
    acc[...] = jnp.zeros_like(acc)

    def body(i, carry):
        load(i).wait()
        s = sketch(i)
        acc[...] += gram_term(i - 1)
        keep(i, s)
        return carry

    lax.fori_loop(1, steps, body, 0)
    acc[...] += gram_term(steps - 1)

    share = rank // n_in
    pl.semaphore_wait(barrier, n_in + n_out - 2)
    mine = pl.ds(pl.multiple_of(me_in * share, share), share)
    sent = []
    copies = []
    for d in range(1, n_in):
        theirs = pl.ds(pl.multiple_of(in_peers[d] * share, share), share)
        copies.append(remote(acc.at[theirs, :], recv1.at[d], s1.at[d], r1.at[d], (in_peers[d], me_out)))
    sent += copies
    total = acc[mine, :]
    for d in range(1, n_in):
        copies[d - 1].wait_recv()
        total = total + recv1[d]
    recv2[me_out] = total
    copies = []
    for d in range(1, n_out):
        copies.append(remote(recv2.at[me_out], recv2.at[me_out], s2.at[d], r2.at[d], (me_in, out_peers[d])))
    sent += copies
    for c in copies:
        c.wait_recv()
    total = recv2[0]
    for d in range(1, n_out):
        total = total + recv2[d]
    whole[mine, :] = total
    copies = []
    for d in range(1, n_in):
        copies.append(remote(whole.at[mine, :], whole.at[mine, :], s3.at[d], r3.at[d], (in_peers[d], me_out)))
    sent += copies
    for c in copies:
        c.wait_recv()

    def flipped(r):
        index = me_in
        for b in range(bits):
            if r >> b & 1:
                bit = lax.rem(me_in // (1 << b), 2)
                index = index + (1 - 2 * bit) * (1 << b)
        return index

    def by_far(count):
        return sorted(range(count), key=lambda r: (-bin(r).count("1"), r))

    peers = [flipped(1 << b) for b in range(bits)]
    order = by_far(n_in // 2)
    way = [list(range(1, bits)), list(range(bits - 1, 0, -1))]
    piece = block // 2
    pending = {}
    used = {}

    def landing(h, w, stage, target):
        if stage == rounds - 1:
            return final.at[h, pl.ds(w * piece, piece), :]
        return stages.at[h, w, (n_in // 2) - (n_in >> (stage + 1)) + target]

    def send_piece(h, w, stage, index, src):
        remaining = sorted(way[w][stage:])
        b = way[w][stage]
        at = remaining.index(b)
        if index >> at & 1:
            target = (index >> (at + 1) << at) | (index & ((1 << at) - 1))
            k = used.get((h, w), 0)
            used[h, w] = k + 1
            copy = remote(
                src, landing(h, w, stage, target), sw.at[h, w, k], rw.at[h, w, k], (peers[b], me_out)
            )
            pending[h, w, stage, target] = copy
            sent.append(copy)

    def product(h, r):
        start = pl.multiple_of(flipped(r) * block, block)
        return dot(basis[h * half : (h + 1) * half, :], ebuf[:, pl.ds(start, block)]).T

    def others(h):
        for r in order:
            part[h, r] = product(h, 2 * r + 1)
            copy = remote(part.at[h, r], first.at[h, r], sc.at[h, r], rc.at[h, r], (peers[0], me_out))
            pending[h, r] = copy
            sent.append(copy)

    def own(h):
        for r in order:
            value = product(h, 2 * r)
            pending[h, r].wait_recv()
            first[h, r] = first[h, r] + value
            for w in (0, 1):
                send_piece(h, w, 0, r, first.at[h, r, pl.ds(w * piece, piece), :])

    def fold(h, stage):
        for w in (0, 1):
            remaining = sorted(way[w][stage:])
            at = remaining.index(way[w][stage])
            for target in by_far(1 << (len(remaining) - 1)):
                index = (target >> at << (at + 1)) | (target & ((1 << at) - 1))
                pending[h, w, stage, target].wait_recv()
                if stage == 0:
                    kept = first[h, index, w * piece : (w + 1) * piece, :]
                else:
                    kept = landing(h, w, stage - 1, index)[...]
                here = landing(h, w, stage, target)
                here[...] = here[...] + kept
                if stage + 1 < rounds:
                    send_piece(h, w, stage + 1, target, here)

    def spread(h):
        for d in range(1, n_out):
            theirs = pl.ds(pl.multiple_of(out_peers[d] * out_block, out_block), out_block)
            copy = remote(
                final.at[h, theirs, :], last.at[h, me_out], sz.at[h, d], rz.at[h, d], (me_in, out_peers[d])
            )
            pending[h, "z", d] = copy
            sent.append(copy)
        here = pl.ds(pl.multiple_of(me_out * out_block, out_block), out_block)
        last[h, me_out] = final[h, here, :]

    def finish(h):
        for d in range(1, n_out):
            pending[h, "z", d].wait_recv()
        total = last[h, 0]
        for d in range(1, n_out):
            total = total + last[h, d]
        out_ref[:, h * half : (h + 1) * half] = total

    def make_basis(h, left, depth):
        for c in range(0, rows, 512):
            basis[h * half : (h + 1) * half, c : c + 512] = dot(
                left, st[:depth, c : c + 512], HIGHEST
            ).astype(jnp.bfloat16)

    def store_at(at):
        def store(base, value):
            m[at + base : at + base + 8, at : at + half] = value
        return store

    sweep(whole[:half, :half], store_at(0))
    upper = m[:half, :half]
    make_basis(0, upper, half)
    others(0)
    own(0)
    x = dot(m[:half, :half], whole[:half, half:], HIGHEST)
    sweep(whole[half:, half:] - dot(x.T, x, HIGHEST), store_at(half))
    fold(0, 0)
    y = dot(x.T, m[:half, :half], HIGHEST)
    m[half:, :half] = -dot(m[half:, half:], y, HIGHEST)
    make_basis(1, m[half:, :], rank)
    others(1)
    for stage in range(1, rounds):
        fold(0, stage)
    spread(0)
    own(1)
    for stage in range(rounds):
        fold(1, stage)
    spread(1)
    finish(0)
    finish(1)
    for c in sent:
        c.wait_send()


def local(n_in, n_out, embedding, test_matrix):
    rows, width = embedding.shape
    rank = test_matrix.shape[1]
    half = rank // 2
    block = width // n_in
    share = rank // n_in
    dma = pltpu.SemaphoreType.DMA
    f32 = jnp.float32
    return pl.pallas_call(
        functools.partial(kernel, n_in, n_out),
        out_shape=jax.ShapeDtypeStruct((block // n_out, rank), f32),
        in_specs=[pl.BlockSpec(memory_space=pl.ANY)] * 2,
        out_specs=pl.BlockSpec(memory_space=pltpu.VMEM),
        scratch_shapes=[
            pltpu.VMEM((rows, width), jnp.bfloat16),
            pltpu.VMEM((width, rank), jnp.bfloat16),
            pltpu.VMEM((CHUNK, rank), f32),
            pltpu.VMEM((rank, rows), f32),
            pltpu.VMEM((rank, rows), jnp.bfloat16),
            pltpu.VMEM((rank, rank), f32),
            pltpu.VMEM((rank, rank), f32),
            pltpu.VMEM((n_in, share, rank), f32),
            pltpu.VMEM((n_out, share, rank), f32),
            pltpu.VMEM((rank, rank), f32),
            pltpu.VMEM((2, n_in // 2, block, half), f32),
            pltpu.VMEM((2, n_in // 2, block, half), f32),
            pltpu.VMEM((2, 2, n_in // 2 - 1, block // 2, half), f32),
            pltpu.VMEM((2, block, half), f32),
            pltpu.VMEM((2, n_out, block // n_out, half), f32),
            dma((rows // CHUNK,)), dma,
            dma((n_in,)), dma((n_in,)), dma((n_out,)), dma((n_out,)), dma((n_in,)), dma((n_in,)),
            dma((2, n_in // 2)), dma((2, n_in // 2)),
            dma((2, 2, n_in // 2)), dma((2, 2, n_in // 2)),
            dma((2, n_out)), dma((2, n_out)),
        ],
        compiler_params=pltpu.CompilerParams(
            collective_id=0, has_side_effects=True, vmem_limit_bytes=VMEM_LIMIT,
        ),
        cost_estimate=pl.CostEstimate(
            flops=4 * rows * width * rank, bytes_accessed=rows * width * 2, transcendentals=0
        ),
    )(embedding, test_matrix)


def solution(mesh):
    n_in, n_out = mesh.shape["inner"], mesh.shape["outer"]
    return jax.shard_map(
        functools.partial(local, n_in, n_out),
        mesh=mesh,
        in_specs=(P(("inner", "outer"), None), P()),
        out_specs=P(("inner", "outer"), None),
        check_vma=False,
    )
```

```python
import functools

import jax
import jax.numpy as jnp
from jax import lax
from jax.experimental import pallas as pl
from jax.experimental.pallas import tpu as pltpu
from jax.sharding import PartitionSpec as P

MESH = pl.DeviceIdType.MESH
HIGHEST = lax.Precision.HIGHEST
VMEM_LIMIT = 58 * 1024 * 1024
CHUNK = 384


def dot(a, b, precision=None):
    return jnp.dot(a, b, precision=precision, preferred_element_type=jnp.float32)


def remote(src, dst, send, recv, device):
    copy = pltpu.make_async_remote_copy(
        src_ref=src, dst_ref=dst, send_sem=send, recv_sem=recv,
        device_id=device, device_id_type=MESH,
    )
    copy.start()
    return copy


def sweep(a, store):
    n = a.shape[0]
    groups = n // 8
    lane = lax.broadcasted_iota(jnp.int32, (8, n), 1)
    sub = lax.broadcasted_iota(jnp.int32, (8, n), 0)
    full = (8, n)
    t = [a[8 * i : 8 * i + 8, :] for i in range(groups)]
    for g in range(groups):
        base = 8 * g
        panel = (lane >= base) & (lane < base + 8)
        cols = [jnp.broadcast_to(t[g][:, base + k : base + k + 1], full) for k in range(8)]
        top = jnp.where(panel, 0.0, t[g])
        scaled, splats, pivots = [], [], None
        for k in range(8):
            pivot = jnp.broadcast_to(cols[k][k : k + 1, :], full)
            inv = 1.0 / pivot
            row = jnp.broadcast_to(top[k : k + 1, :], full)
            scaled.append(jnp.where(lane == base + k, inv, row * inv))
            splat = {l: jnp.broadcast_to(cols[l][k : k + 1, :], full) * inv for l in range(k + 1, 8)}
            splats.append(splat)
            pivots = pivot if k == 0 else jnp.where(sub >= k, pivot, pivots)
            if k < 7:
                below = jnp.where(sub > k, cols[k], 0.0)
                for l in range(k + 1, 8):
                    cols[l] = cols[l] - below * splat[l]
                top = top - below * scaled[k]
        rows = jnp.where(lane == base + sub, 1.0, jnp.where(lane < base + 8, top, 0.0))
        store(base, rows / jnp.sqrt(pivots))
        for first in range(g + 1, groups, 4):
            those = range(first, min(first + 4, groups))
            old = jnp.stack([t[i] for i in those])
            c = [jnp.broadcast_to(old[:, :, base + k : base + k + 1], old.shape) for k in range(8)]
            x = jnp.where(panel, 0.0, old)
            for k in range(8):
                for l in range(k + 1, 8):
                    c[l] = c[l] - c[k] * splats[k][l]
                x = x - c[k] * scaled[k]
            for at, i in enumerate(those):
                t[i] = x[at]
        yield


def kernel(
    n_in, n_out, e_ref, t_ref, out_ref,
    ebuf, tbuf, left1, left2, right1, right2, st, basis, acc1, acc2, m,
    recv1_a, recv2_a, whole_a, recv1_b, recv2_b, whole_b,
    part, first, stages, final, last,
    esem, tsem, s1, r1, s2, r2, s3, r3, sc, rc, sw, rw, sz, rz,
):
    me_in, me_out = lax.axis_index("inner"), lax.axis_index("outer")
    rows, width = ebuf.shape
    rank = acc1.shape[0]
    half = rank // 2
    bits = n_in.bit_length() - 1
    rounds = bits - 1
    block = width // n_in
    out_block = block // n_out
    steps = rows // CHUNK

    barrier = pltpu.get_barrier_semaphore()
    in_peers = [lax.rem(me_in + d, n_in) for d in range(n_in)]
    out_peers = [lax.rem(me_out + d, n_out) for d in range(n_out)]
    for d in range(1, n_in):
        pl.semaphore_signal(barrier, inc=1, device_id=(in_peers[d], me_out), device_id_type=MESH)
    for d in range(1, n_out):
        pl.semaphore_signal(barrier, inc=1, device_id=(me_in, out_peers[d]), device_id_type=MESH)

    test_copy = pltpu.make_async_copy(t_ref, tbuf, tsem)
    test_copy.start()

    def load(i):
        span = pl.ds(pl.multiple_of(i * CHUNK, CHUNK), CHUNK)
        return pltpu.make_async_copy(e_ref.at[span, :], ebuf.at[span, :], esem.at[i])

    for i in range(steps):
        load(i).start()

    def sketch(i):
        span = pl.ds(pl.multiple_of(i * CHUNK, CHUNK), CHUNK)
        return dot(ebuf[span, :], tbuf[...])

    def split(value):
        high = value.astype(jnp.bfloat16)
        rest = value - high.astype(jnp.float32)
        middle = rest.astype(jnp.bfloat16)
        return high, middle, (rest - middle.astype(jnp.float32)).astype(jnp.bfloat16)

    def keep(i, s):
        span = pl.ds(pl.multiple_of(i * CHUNK, CHUNK), CHUNK)
        t = s.T
        st[:, span] = t
        high, middle, low = split(s)
        right1[:CHUNK, :] = high
        right1[CHUNK:, :] = middle
        right2[:CHUNK, :] = middle
        right2[CHUNK:, :] = low
        high, middle, low = split(t)
        left1[:, :CHUNK] = high
        left1[:, CHUNK:] = middle
        left2[:, :CHUNK] = high
        left2[:, CHUNK:] = high

    def gram_term():
        acc1[...] += dot(left1[...], right1[...])
        acc2[...] += dot(left2[...], right2[...])

    test_copy.wait()
    load(0).wait()
    keep(0, sketch(0))
    acc1[...] = jnp.zeros_like(acc1)
    acc2[...] = jnp.zeros_like(acc2)

    def body(i, carry):
        load(i).wait()
        s = sketch(i)
        gram_term()
        keep(i, s)
        return carry

    lax.fori_loop(1, steps, body, 0)
    gram_term()
    acc1[...] = acc1[...] + acc2[...] + acc2[...].T

    share = half // n_in
    mine = pl.ds(pl.multiple_of(me_in * share, share), share)
    sent = []

    class Sum:
        def __init__(self, at, row, lanes, recv1, recv2, whole):
            self.at, self.row, self.lanes = at, row, lanes
            self.recv1, self.recv2, self.whole = recv1, recv2, whole

        def rows_of(self, peer):
            start = pl.multiple_of(self.row + peer * share, share)
            return acc1.at[pl.ds(start, share), pl.ds(0, self.lanes)]

        def start(self):
            self.copies = [
                remote(
                    self.rows_of(in_peers[d]), self.recv1.at[d],
                    s1.at[self.at, d], r1.at[self.at, d], (in_peers[d], me_out),
                )
                for d in range(1, n_in)
            ]
            sent.extend(self.copies)

        def exchange(self):
            total = self.rows_of(me_in)[...]
            for d in range(1, n_in):
                self.copies[d - 1].wait_recv()
                total = total + self.recv1[d]
            self.recv2[me_out] = total
            self.copies = [
                remote(
                    self.recv2.at[me_out], self.recv2.at[me_out],
                    s2.at[self.at, d], r2.at[self.at, d], (me_in, out_peers[d]),
                )
                for d in range(1, n_out)
            ]
            sent.extend(self.copies)

        def gather(self):
            for c in self.copies:
                c.wait_recv()
            total = self.recv2[0]
            for d in range(1, n_out):
                total = total + self.recv2[d]
            self.whole[mine, :] = total
            self.copies = [
                remote(
                    self.whole.at[mine, :], self.whole.at[mine, :],
                    s3.at[self.at, d], r3.at[self.at, d], (in_peers[d], me_out),
                )
                for d in range(1, n_in)
            ]
            sent.extend(self.copies)

        def done(self):
            for c in self.copies:
                c.wait_recv()

    sum_a = Sum(0, 0, half, recv1_a, recv2_a, whole_a)
    sum_b = Sum(1, half, rank, recv1_b, recv2_b, whole_b)
    pl.semaphore_wait(barrier, n_in + n_out - 2)
    sum_a.start()
    sum_b.start()
    sum_a.exchange()
    sum_b.exchange()
    sum_a.gather()
    sum_a.done()

    def flipped(r):
        index = me_in
        for b in range(bits):
            if r >> b & 1:
                bit = lax.rem(me_in // (1 << b), 2)
                index = index + (1 - 2 * bit) * (1 << b)
        return index

    def by_far(count):
        return sorted(range(count), key=lambda r: (-bin(r).count("1"), r))

    peers = [flipped(1 << b) for b in range(bits)]
    order = by_far(n_in // 2)
    way = [list(range(1, bits)), list(range(bits - 1, 0, -1))]
    piece = block // 2
    pending = {}
    used = {}

    def landing(h, w, stage, target):
        if stage == rounds - 1:
            return final.at[h, pl.ds(w * piece, piece), :]
        return stages.at[h, w, (n_in // 2) - (n_in >> (stage + 1)) + target]

    def send_piece(h, w, stage, index, src):
        remaining = sorted(way[w][stage:])
        b = way[w][stage]
        at = remaining.index(b)
        if index >> at & 1:
            target = (index >> (at + 1) << at) | (index & ((1 << at) - 1))
            k = used.get((h, w), 0)
            used[h, w] = k + 1
            copy = remote(
                src, landing(h, w, stage, target), sw.at[h, w, k], rw.at[h, w, k], (peers[b], me_out)
            )
            pending[h, w, stage, target] = copy
            sent.append(copy)

    def product(h, r):
        start = pl.multiple_of(flipped(r) * block, block)
        return dot(basis[h * half : (h + 1) * half, :], ebuf[:, pl.ds(start, block)]).T

    def others(h, beside):
        for r in order:
            part[h, r] = product(h, 2 * r + 1)
            beside()
            copy = remote(part.at[h, r], first.at[h, r], sc.at[h, r], rc.at[h, r], (peers[0], me_out))
            pending[h, r] = copy
            sent.append(copy)

    def own(h, beside):
        for r in order:
            value = product(h, 2 * r)
            beside()
            pending[h, r].wait_recv()
            first[h, r] = first[h, r] + value
            for w in (0, 1):
                send_piece(h, w, 0, r, first.at[h, r, pl.ds(w * piece, piece), :])

    def fold(h, stage):
        count = 1 << (len(way[0][stage:]) - 1)
        for target in by_far(count):
            for w in (0, 1):
                at = sorted(way[w][stage:]).index(way[w][stage])
                index = (target >> at << (at + 1)) | (target & ((1 << at) - 1))
                pending[h, w, stage, target].wait_recv()
                if stage == 0:
                    kept = first[h, index, w * piece : (w + 1) * piece, :]
                else:
                    kept = landing(h, w, stage - 1, index)[...]
                here = landing(h, w, stage, target)
                here[...] = here[...] + kept
                if stage + 1 < rounds:
                    send_piece(h, w, stage + 1, target, here)

    def spread(h):
        for d in range(1, n_out):
            theirs = pl.ds(pl.multiple_of(out_peers[d] * out_block, out_block), out_block)
            copy = remote(
                final.at[h, theirs, :], last.at[h, me_out], sz.at[h, d], rz.at[h, d], (me_in, out_peers[d])
            )
            pending[h, "z", d] = copy
            sent.append(copy)
        here = pl.ds(pl.multiple_of(me_out * out_block, out_block), out_block)
        last[h, me_out] = final[h, here, :]

    def finish(h):
        for d in range(1, n_out):
            pending[h, "z", d].wait_recv()
        total = last[h, 0]
        for d in range(1, n_out):
            total = total + last[h, d]
        out_ref[:, h * half : (h + 1) * half] = total

    def make_basis(h, left, depth):
        for c in range(0, rows, 512):
            basis[h * half : (h + 1) * half, c : c + 512] = dot(
                left, st[:depth, c : c + 512], HIGHEST
            ).astype(jnp.bfloat16)

    def store_at(at):
        def store(base, value):
            m[at + base : at + base + 8, at : at + half] = value
        return store

    panels = half // 8
    for panel, _ in enumerate(sweep(whole_a[...], store_at(0))):
        if panel == panels // 2:
            sum_b.gather()
    make_basis(0, m[:half, :half], half)
    sum_b.done()
    x = dot(m[:half, :half], whole_b[:, :half].T, HIGHEST)
    second = sweep(whole_b[:, half:] - dot(x.T, x, HIGHEST), store_at(half))

    def advance():
        for _ in range(panels // n_in):
            next(second, None)

    def nothing():
        pass

    others(0, advance)
    own(0, advance)
    for _ in second:
        pass
    fold(0, 0)
    y = dot(x.T, m[:half, :half], HIGHEST)
    m[half:, :half] = -dot(m[half:, half:], y, HIGHEST)
    make_basis(1, m[half:, :], rank)
    others(1, nothing)
    for stage in range(1, rounds):
        fold(0, stage)
    spread(0)
    own(1, nothing)
    for stage in range(rounds):
        fold(1, stage)
    spread(1)
    finish(0)
    finish(1)
    for c in sent:
        c.wait_send()


def local(n_in, n_out, embedding, test_matrix):
    rows, width = embedding.shape
    rank = test_matrix.shape[1]
    half = rank // 2
    block = width // n_in
    share = half // n_in
    dma = pltpu.SemaphoreType.DMA
    f32 = jnp.float32
    return pl.pallas_call(
        functools.partial(kernel, n_in, n_out),
        out_shape=jax.ShapeDtypeStruct((block // n_out, rank), f32),
        in_specs=[pl.BlockSpec(memory_space=pl.ANY)] * 2,
        out_specs=pl.BlockSpec(memory_space=pltpu.VMEM),
        scratch_shapes=[
            pltpu.VMEM((rows, width), jnp.bfloat16),
            pltpu.VMEM((width, rank), jnp.bfloat16),
            pltpu.VMEM((rank, 2 * CHUNK), jnp.bfloat16),
            pltpu.VMEM((rank, 2 * CHUNK), jnp.bfloat16),
            pltpu.VMEM((2 * CHUNK, rank), jnp.bfloat16),
            pltpu.VMEM((2 * CHUNK, rank), jnp.bfloat16),
            pltpu.VMEM((rank, rows), f32),
            pltpu.VMEM((rank, rows), jnp.bfloat16),
            pltpu.VMEM((rank, rank), f32),
            pltpu.VMEM((rank, rank), f32),
            pltpu.VMEM((rank, rank), f32),
            pltpu.VMEM((n_in, share, half), f32),
            pltpu.VMEM((n_out, share, half), f32),
            pltpu.VMEM((half, half), f32),
            pltpu.VMEM((n_in, share, rank), f32),
            pltpu.VMEM((n_out, share, rank), f32),
            pltpu.VMEM((half, rank), f32),
            pltpu.VMEM((2, n_in // 2, block, half), f32),
            pltpu.VMEM((2, n_in // 2, block, half), f32),
            pltpu.VMEM((2, 2, n_in // 2 - 1, block // 2, half), f32),
            pltpu.VMEM((2, block, half), f32),
            pltpu.VMEM((2, n_out, block // n_out, half), f32),
            dma((rows // CHUNK,)), dma,
            dma((2, n_in)), dma((2, n_in)), dma((2, n_out)), dma((2, n_out)), dma((2, n_in)), dma((2, n_in)),
            dma((2, n_in // 2)), dma((2, n_in // 2)),
            dma((2, 2, n_in // 2)), dma((2, 2, n_in // 2)),
            dma((2, n_out)), dma((2, n_out)),
        ],
        compiler_params=pltpu.CompilerParams(
            collective_id=0, has_side_effects=True, vmem_limit_bytes=VMEM_LIMIT,
        ),
        cost_estimate=pl.CostEstimate(
            flops=4 * rows * width * rank, bytes_accessed=rows * width * 2, transcendentals=0
        ),
    )(embedding, test_matrix)


def solution(mesh):
    n_in, n_out = mesh.shape["inner"], mesh.shape["outer"]
    return jax.shard_map(
        functools.partial(local, n_in, n_out),
        mesh=mesh,
        in_specs=(P(("inner", "outer"), None), P()),
        out_specs=P(("inner", "outer"), None),
        check_vma=False,
    )
```

```python
import functools

import jax
import jax.numpy as jnp
from jax import lax
from jax.experimental import pallas as pl
from jax.experimental.pallas import tpu as pltpu
from jax.sharding import PartitionSpec as P

MESH = pl.DeviceIdType.MESH
HIGHEST = lax.Precision.HIGHEST
VMEM_LIMIT = 58 * 1024 * 1024
CHUNK = 256
AHEAD = 4


def dot(a, b, precision=None):
    return jnp.dot(a, b, precision=precision, preferred_element_type=jnp.float32)


def remote(src, dst, send, recv, device):
    copy = pltpu.make_async_remote_copy(
        src_ref=src, dst_ref=dst, send_sem=send, recv_sem=recv,
        device_id=device, device_id_type=MESH,
    )
    copy.start()
    return copy


def sweep(a, store):
    n = a.shape[0]
    groups = n // 8
    lane = lax.broadcasted_iota(jnp.int32, (8, n), 1)
    sub = lax.broadcasted_iota(jnp.int32, (8, n), 0)
    full = (8, n)
    t = [a[8 * i : 8 * i + 8, :] for i in range(groups)]
    for g in range(groups):
        base = 8 * g
        panel = (lane >= base) & (lane < base + 8)
        cols = [jnp.broadcast_to(t[g][:, base + k : base + k + 1], full) for k in range(8)]
        top = jnp.where(panel, 0.0, t[g])
        scaled, splats, pivots = [], [], None
        for k in range(8):
            pivot = jnp.broadcast_to(cols[k][k : k + 1, :], full)
            inv = 1.0 / pivot
            row = jnp.broadcast_to(top[k : k + 1, :], full)
            scaled.append(jnp.where(lane == base + k, inv, row * inv))
            splat = {l: jnp.broadcast_to(cols[l][k : k + 1, :], full) * inv for l in range(k + 1, 8)}
            splats.append(splat)
            pivots = pivot if k == 0 else jnp.where(sub >= k, pivot, pivots)
            if k < 7:
                below = jnp.where(sub > k, cols[k], 0.0)
                for l in range(k + 1, 8):
                    cols[l] = cols[l] - below * splat[l]
                top = top - below * scaled[k]
        rows = jnp.where(lane == base + sub, 1.0, jnp.where(lane < base + 8, top, 0.0))
        store(base, rows / jnp.sqrt(pivots))
        for first in range(g + 1, groups, 4):
            those = range(first, min(first + 4, groups))
            old = jnp.stack([t[i] for i in those])
            c = [jnp.broadcast_to(old[:, :, base + k : base + k + 1], old.shape) for k in range(8)]
            x = jnp.where(panel, 0.0, old)
            for k in range(8):
                for l in range(k + 1, 8):
                    c[l] = c[l] - c[k] * splats[k][l]
                x = x - c[k] * scaled[k]
            for at, i in enumerate(those):
                t[i] = x[at]
        yield


def kernel(
    n_in, n_out, e_ref, t_ref, out_ref,
    ebuf, tbuf, left1, left2, right1, right2, st, basis, acc1, acc2, m,
    recv1_a, recv2_a, whole_a, recv1_b, recv2_b, whole_b,
    part, first, stages, final, last,
    esem, tsem, s1, r1, s2, r2, s3, r3, sc, rc, sw, rw, sz, rz,
):
    me_in, me_out = lax.axis_index("inner"), lax.axis_index("outer")
    rows, width = ebuf.shape
    rank = acc1.shape[0]
    half = rank // 2
    bits = n_in.bit_length() - 1
    rounds = bits - 1
    block = width // n_in
    out_block = block // n_out
    steps = rows // CHUNK

    barrier = pltpu.get_barrier_semaphore()
    in_peers = [lax.rem(me_in + d, n_in) for d in range(n_in)]
    out_peers = [lax.rem(me_out + d, n_out) for d in range(n_out)]
    for d in range(1, n_in):
        pl.semaphore_signal(barrier, inc=1, device_id=(in_peers[d], me_out), device_id_type=MESH)
    for d in range(1, n_out):
        pl.semaphore_signal(barrier, inc=1, device_id=(me_in, out_peers[d]), device_id_type=MESH)

    test_copy = pltpu.make_async_copy(t_ref, tbuf, tsem)
    test_copy.start()

    def load(i):
        span = pl.ds(pl.multiple_of(i * CHUNK, CHUNK), CHUNK)
        return pltpu.make_async_copy(e_ref.at[span, :], ebuf.at[span, :], esem.at[i])

    for i in range(AHEAD):
        load(i).start()

    def sketch(i):
        span = pl.ds(pl.multiple_of(i * CHUNK, CHUNK), CHUNK)
        return dot(ebuf[span, :], tbuf[...])

    def split(value):
        high = value.astype(jnp.bfloat16)
        rest = value - high.astype(jnp.float32)
        middle = rest.astype(jnp.bfloat16)
        return high, middle, (rest - middle.astype(jnp.float32)).astype(jnp.bfloat16)

    def keep(i, s):
        span = pl.ds(pl.multiple_of(i * CHUNK, CHUNK), CHUNK)
        t = s.T
        st[:, span] = t
        high, middle, low = split(s)
        right1[:CHUNK, :] = high
        right1[CHUNK:, :] = middle
        right2[:CHUNK, :] = middle
        right2[CHUNK:, :] = low
        high, middle, low = split(t)
        left1[:, :CHUNK] = high
        left1[:, CHUNK:] = middle
        left2[:, :CHUNK] = high
        left2[:, CHUNK:] = high

    def gram_term():
        acc1[...] += dot(left1[...], right1[...])
        acc2[...] += dot(left2[...], right2[...])

    test_copy.wait()
    load(0).wait()
    load(AHEAD).start()
    keep(0, sketch(0))
    acc1[...] = jnp.zeros_like(acc1)
    acc2[...] = jnp.zeros_like(acc2)

    def body(i, carry):
        load(i).wait()

        @pl.when(i + AHEAD < steps)
        def _():
            load(i + AHEAD).start()

        s = sketch(i)
        gram_term()
        keep(i, s)
        return carry

    lax.fori_loop(1, steps, body, 0)
    gram_term()
    acc1[...] = acc1[...] + acc2[...] + acc2[...].T

    share = half // n_in
    mine = pl.ds(pl.multiple_of(me_in * share, share), share)
    sent = []

    class Sum:
        def __init__(self, at, row, lanes, recv1, recv2, whole):
            self.at, self.row, self.lanes = at, row, lanes
            self.recv1, self.recv2, self.whole = recv1, recv2, whole

        def rows_of(self, peer):
            start = pl.multiple_of(self.row + peer * share, share)
            return acc1.at[pl.ds(start, share), pl.ds(0, self.lanes)]

        def start(self):
            self.copies = [
                remote(
                    self.rows_of(in_peers[d]), self.recv1.at[d],
                    s1.at[self.at, d], r1.at[self.at, d], (in_peers[d], me_out),
                )
                for d in range(1, n_in)
            ]
            sent.extend(self.copies)

        def exchange(self):
            total = self.rows_of(me_in)[...]
            for d in range(1, n_in):
                self.copies[d - 1].wait_recv()
                total = total + self.recv1[d]
            self.recv2[me_out] = total
            self.copies = [
                remote(
                    self.recv2.at[me_out], self.recv2.at[me_out],
                    s2.at[self.at, d], r2.at[self.at, d], (me_in, out_peers[d]),
                )
                for d in range(1, n_out)
            ]
            sent.extend(self.copies)

        def gather(self):
            for c in self.copies:
                c.wait_recv()
            total = self.recv2[0]
            for d in range(1, n_out):
                total = total + self.recv2[d]
            self.whole[mine, :] = total
            self.copies = [
                remote(
                    self.whole.at[mine, :], self.whole.at[mine, :],
                    s3.at[self.at, d], r3.at[self.at, d], (in_peers[d], me_out),
                )
                for d in range(1, n_in)
            ]
            sent.extend(self.copies)

        def done(self):
            for c in self.copies:
                c.wait_recv()

    sum_a = Sum(0, 0, half, recv1_a, recv2_a, whole_a)
    sum_b = Sum(1, half, rank, recv1_b, recv2_b, whole_b)
    pl.semaphore_wait(barrier, n_in + n_out - 2)
    sum_a.start()
    sum_b.start()
    sum_a.exchange()
    sum_b.exchange()
    sum_a.gather()
    sum_a.done()

    def flipped(r):
        index = me_in
        for b in range(bits):
            if r >> b & 1:
                bit = lax.rem(me_in // (1 << b), 2)
                index = index + (1 - 2 * bit) * (1 << b)
        return index

    def by_far(count):
        return sorted(range(count), key=lambda r: (-bin(r).count("1"), r))

    peers = [flipped(1 << b) for b in range(bits)]
    order = by_far(n_in // 2)
    up, down = list(range(1, bits)), list(range(bits - 1, 0, -1))
    way = [up if d % 2 else down for d in range(n_out)]
    turns = list(range(1, n_out)) + [0]

    def rows_for(d):
        return pl.ds(pl.multiple_of(out_peers[d] * out_block, out_block), out_block)

    pending = {}
    used = {}

    def landing(h, w, stage, target):
        if stage == rounds - 1:
            return final.at[h, w]
        return stages.at[h, w, (n_in // 2) - (n_in >> (stage + 1)) + target]

    def send_piece(h, w, stage, index, src):
        remaining = sorted(way[w][stage:])
        b = way[w][stage]
        at = remaining.index(b)
        if index >> at & 1:
            target = (index >> (at + 1) << at) | (index & ((1 << at) - 1))
            k = used.get((h, w), 0)
            used[h, w] = k + 1
            copy = remote(
                src, landing(h, w, stage, target), sw.at[h, w, k], rw.at[h, w, k], (peers[b], me_out)
            )
            pending[h, w, stage, target] = copy
            sent.append(copy)

    def product(h, r):
        start = pl.multiple_of(flipped(r) * block, block)
        return dot(basis[h * half : (h + 1) * half, :], ebuf[:, pl.ds(start, block)]).T

    def others(h):
        for r in order:
            part[h, r] = product(h, 2 * r + 1)
            copy = remote(part.at[h, r], first.at[h, r], sc.at[h, r], rc.at[h, r], (peers[0], me_out))
            pending[h, r] = copy
            sent.append(copy)

    def own(h):
        for r in order:
            value = product(h, 2 * r)
            pending[h, r].wait_recv()
            first[h, r] = first[h, r] + value
            for w in turns:
                send_piece(h, w, 0, r, first.at[h, r, rows_for(w), :])

    def fold(h, stage):
        count = 1 << (len(way[0][stage:]) - 1)
        for target in by_far(count):
            for w in turns:
                at = sorted(way[w][stage:]).index(way[w][stage])
                index = (target >> at << (at + 1)) | (target & ((1 << at) - 1))
                pending[h, w, stage, target].wait_recv()
                if stage == 0:
                    kept = first[h, index, rows_for(w), :]
                else:
                    kept = landing(h, w, stage - 1, index)[...]
                here = landing(h, w, stage, target)
                here[...] = here[...] + kept
                if stage + 1 < rounds:
                    send_piece(h, w, stage + 1, target, here)
                elif w:
                    copy = remote(
                        here, last.at[h, me_out], sz.at[h, w], rz.at[h, w], (me_in, out_peers[w])
                    )
                    pending[h, "z", w] = copy
                    sent.append(copy)
                else:
                    last[h, me_out] = here[...]

    def finish(h):
        for d in range(1, n_out):
            pending[h, "z", d].wait_recv()
        total = last[h, 0]
        for d in range(1, n_out):
            total = total + last[h, d]
        out_ref[:, h * half : (h + 1) * half] = total

    def make_basis(h, left, depth):
        for c in range(0, rows, 512):
            basis[h * half : (h + 1) * half, c : c + 512] = dot(
                left, st[:depth, c : c + 512], HIGHEST
            ).astype(jnp.bfloat16)

    def store_at(at):
        def store(base, value):
            m[at + base : at + base + 8, at : at + half] = value
        return store

    panels = half // 8
    for panel, _ in enumerate(sweep(whole_a[...], store_at(0))):
        if panel == panels // 2:
            sum_b.gather()
    make_basis(0, m[:half, :half], half)
    others(0)
    own(0)
    sum_b.done()
    x = dot(m[:half, :half], whole_b[:, :half].T, HIGHEST)
    second = sweep(whole_b[:, half:] - dot(x.T, x, HIGHEST), store_at(half))

    for panel, _ in enumerate(second):
        if panel == 5 * panels // 8:
            fold(0, 0)
    y = dot(x.T, m[:half, :half], HIGHEST)
    m[half:, :half] = -dot(m[half:, half:], y, HIGHEST)
    make_basis(1, m[half:, :], rank)
    for stage in range(1, rounds):
        fold(0, stage)
    others(1)
    own(1)
    for stage in range(rounds):
        fold(1, stage)
    finish(0)
    finish(1)
    for c in sent:
        c.wait_send()


def local(n_in, n_out, embedding, test_matrix):
    rows, width = embedding.shape
    rank = test_matrix.shape[1]
    half = rank // 2
    block = width // n_in
    share = half // n_in
    dma = pltpu.SemaphoreType.DMA
    f32 = jnp.float32
    return pl.pallas_call(
        functools.partial(kernel, n_in, n_out),
        out_shape=jax.ShapeDtypeStruct((block // n_out, rank), f32),
        in_specs=[pl.BlockSpec(memory_space=pl.ANY)] * 2,
        out_specs=pl.BlockSpec(memory_space=pltpu.VMEM),
        scratch_shapes=[
            pltpu.VMEM((rows, width), jnp.bfloat16),
            pltpu.VMEM((width, rank), jnp.bfloat16),
            pltpu.VMEM((rank, 2 * CHUNK), jnp.bfloat16),
            pltpu.VMEM((rank, 2 * CHUNK), jnp.bfloat16),
            pltpu.VMEM((2 * CHUNK, rank), jnp.bfloat16),
            pltpu.VMEM((2 * CHUNK, rank), jnp.bfloat16),
            pltpu.VMEM((rank, rows), f32),
            pltpu.VMEM((rank, rows), jnp.bfloat16),
            pltpu.VMEM((rank, rank), f32),
            pltpu.VMEM((rank, rank), f32),
            pltpu.VMEM((rank, rank), f32),
            pltpu.VMEM((n_in, share, half), f32),
            pltpu.VMEM((n_out, share, half), f32),
            pltpu.VMEM((half, half), f32),
            pltpu.VMEM((n_in, share, rank), f32),
            pltpu.VMEM((n_out, share, rank), f32),
            pltpu.VMEM((half, rank), f32),
            pltpu.VMEM((2, n_in // 2, block, half), f32),
            pltpu.VMEM((2, n_in // 2, block, half), f32),
            pltpu.VMEM((2, n_out, n_in // 2 - 1, block // n_out, half), f32),
            pltpu.VMEM((2, n_out, block // n_out, half), f32),
            pltpu.VMEM((2, n_out, block // n_out, half), f32),
            dma((rows // CHUNK,)), dma,
            dma((2, n_in)), dma((2, n_in)), dma((2, n_out)), dma((2, n_out)), dma((2, n_in)), dma((2, n_in)),
            dma((2, n_in // 2)), dma((2, n_in // 2)),
            dma((2, n_out, n_in // 2)), dma((2, n_out, n_in // 2)),
            dma((2, n_out)), dma((2, n_out)),
        ],
        compiler_params=pltpu.CompilerParams(
            collective_id=0, has_side_effects=True, vmem_limit_bytes=VMEM_LIMIT,
        ),
        cost_estimate=pl.CostEstimate(
            flops=4 * rows * width * rank, bytes_accessed=rows * width * 2, transcendentals=0
        ),
    )(embedding, test_matrix)


def solution(mesh):
    n_in, n_out = mesh.shape["inner"], mesh.shape["outer"]
    return jax.shard_map(
        functools.partial(local, n_in, n_out),
        mesh=mesh,
        in_specs=(P(("inner", "outer"), None), P()),
        out_specs=P(("inner", "outer"), None),
        check_vma=False,
    )
```

```python
import functools

import jax
import jax.numpy as jnp
from jax import lax
from jax.experimental import pallas as pl
from jax.experimental.pallas import tpu as pltpu
from jax.sharding import PartitionSpec as P

MESH = pl.DeviceIdType.MESH
HIGHEST = lax.Precision.HIGHEST
VMEM_LIMIT = 58 * 1024 * 1024
CHUNK = 256
AHEAD = 4


def dot(a, b, precision=None):
    return jnp.dot(a, b, precision=precision, preferred_element_type=jnp.float32)


def remote(src, dst, send, recv, device):
    copy = pltpu.make_async_remote_copy(
        src_ref=src, dst_ref=dst, send_sem=send, recv_sem=recv,
        device_id=device, device_id_type=MESH,
    )
    copy.start()
    return copy


def sweep(a, store):
    n = a.shape[0]
    groups = n // 8
    lane = lax.broadcasted_iota(jnp.int32, (8, n), 1)
    sub = lax.broadcasted_iota(jnp.int32, (8, n), 0)
    full = (8, n)
    t = [a[8 * i : 8 * i + 8, :] for i in range(groups)]
    for g in range(groups):
        base = 8 * g
        panel = (lane >= base) & (lane < base + 8)
        cols = [jnp.broadcast_to(t[g][:, base + k : base + k + 1], full) for k in range(8)]
        top = jnp.where(panel, 0.0, t[g])
        scaled, splats, pivots = [], [], None
        for k in range(8):
            pivot = jnp.broadcast_to(cols[k][k : k + 1, :], full)
            inv = 1.0 / pivot
            row = jnp.broadcast_to(top[k : k + 1, :], full)
            scaled.append(jnp.where(lane == base + k, inv, row * inv))
            splat = {l: jnp.broadcast_to(cols[l][k : k + 1, :], full) * inv for l in range(k + 1, 8)}
            splats.append(splat)
            pivots = pivot if k == 0 else jnp.where(sub >= k, pivot, pivots)
            if k < 7:
                below = jnp.where(sub > k, cols[k], 0.0)
                for l in range(k + 1, 8):
                    cols[l] = cols[l] - below * splat[l]
                top = top - below * scaled[k]
        rows = jnp.where(lane == base + sub, 1.0, jnp.where(lane < base + 8, top, 0.0))
        store(base, rows / jnp.sqrt(pivots))
        for first in range(g + 1, groups, 4):
            those = range(first, min(first + 4, groups))
            old = jnp.stack([t[i] for i in those])
            c = [jnp.broadcast_to(old[:, :, base + k : base + k + 1], old.shape) for k in range(8)]
            x = jnp.where(panel, 0.0, old)
            for k in range(8):
                for l in range(k + 1, 8):
                    c[l] = c[l] - c[k] * splats[k][l]
                x = x - c[k] * scaled[k]
            for at, i in enumerate(those):
                t[i] = x[at]
        yield


def kernel(
    n_in, n_out, e_ref, t_ref, out_ref,
    ebuf, tbuf, left1, left2, right1, right2, st, basis, acc1, acc2, m,
    recv1_a, recv2_a, whole_a, recv1_b, recv2_b, whole_b,
    part, first, stages, final, last,
    esem, tsem, s1, r1, s2, r2, s3, r3, sc, rc, sw, rw, sz, rz,
):
    me_in, me_out = lax.axis_index("inner"), lax.axis_index("outer")
    rows, width = ebuf.shape
    rank = acc1.shape[0]
    half = rank // 2
    bits = n_in.bit_length() - 1
    rounds = bits - 1
    block = width // n_in
    out_block = block // n_out
    steps = rows // CHUNK

    barrier = pltpu.get_barrier_semaphore()
    in_peers = [lax.rem(me_in + d, n_in) for d in range(n_in)]
    out_peers = [lax.rem(me_out + d, n_out) for d in range(n_out)]
    for d in range(1, n_in):
        pl.semaphore_signal(barrier, inc=1, device_id=(in_peers[d], me_out), device_id_type=MESH)
    for d in range(1, n_out):
        pl.semaphore_signal(barrier, inc=1, device_id=(me_in, out_peers[d]), device_id_type=MESH)

    test_copy = pltpu.make_async_copy(t_ref, tbuf, tsem)
    test_copy.start()

    def load(i):
        span = pl.ds(pl.multiple_of(i * CHUNK, CHUNK), CHUNK)
        return pltpu.make_async_copy(e_ref.at[span, :], ebuf.at[span, :], esem.at[i])

    for i in range(AHEAD):
        load(i).start()

    def sketch(i):
        span = pl.ds(pl.multiple_of(i * CHUNK, CHUNK), CHUNK)
        return dot(ebuf[span, :], tbuf[...])

    def split(value):
        high = value.astype(jnp.bfloat16)
        rest = value - high.astype(jnp.float32)
        middle = rest.astype(jnp.bfloat16)
        return high, middle, (rest - middle.astype(jnp.float32)).astype(jnp.bfloat16)

    def keep(i, s):
        span = pl.ds(pl.multiple_of(i * CHUNK, CHUNK), CHUNK)
        t = s.T
        st[:, span] = t
        high, middle, low = split(s)
        right1[:CHUNK, :] = high
        right1[CHUNK:, :] = middle
        right2[:CHUNK, :] = middle
        right2[CHUNK:, :] = low
        high, middle, low = split(t)
        left1[:, :CHUNK] = high
        left1[:, CHUNK:] = middle
        left2[:, :CHUNK] = high
        left2[:, CHUNK:] = high

    def gram_term():
        acc1[...] += dot(left1[...], right1[...])
        acc2[...] += dot(left2[...], right2[...])

    test_copy.wait()
    load(0).wait()
    load(AHEAD).start()
    keep(0, sketch(0))
    acc1[...] = jnp.zeros_like(acc1)
    acc2[...] = jnp.zeros_like(acc2)

    def body(i, carry):
        load(i).wait()

        @pl.when(i + AHEAD < steps)
        def _():
            load(i + AHEAD).start()

        s = sketch(i)
        gram_term()
        keep(i, s)
        return carry

    lax.fori_loop(1, steps, body, 0)
    gram_term()
    acc1[...] = acc1[...] + acc2[...] + acc2[...].T

    share = half // n_in
    mine = pl.ds(pl.multiple_of(me_in * share, share), share)
    sent = []

    class Sum:
        def __init__(self, at, row, lanes, recv1, recv2, whole):
            self.at, self.row, self.lanes = at, row, lanes
            self.recv1, self.recv2, self.whole = recv1, recv2, whole

        def rows_of(self, peer):
            start = pl.multiple_of(self.row + peer * share, share)
            return acc1.at[pl.ds(start, share), pl.ds(0, self.lanes)]

        def start(self):
            self.copies = [
                remote(
                    self.rows_of(in_peers[d]), self.recv1.at[d],
                    s1.at[self.at, d], r1.at[self.at, d], (in_peers[d], me_out),
                )
                for d in range(1, n_in)
            ]
            sent.extend(self.copies)

        def exchange(self):
            total = self.rows_of(me_in)[...]
            for d in range(1, n_in):
                self.copies[d - 1].wait_recv()
                total = total + self.recv1[d]
            self.recv2[me_out] = total
            self.copies = [
                remote(
                    self.recv2.at[me_out], self.recv2.at[me_out],
                    s2.at[self.at, d], r2.at[self.at, d], (me_in, out_peers[d]),
                )
                for d in range(1, n_out)
            ]
            sent.extend(self.copies)

        def gather(self):
            for c in self.copies:
                c.wait_recv()
            total = self.recv2[0]
            for d in range(1, n_out):
                total = total + self.recv2[d]
            self.whole[mine, :] = total
            self.copies = [
                remote(
                    self.whole.at[mine, :], self.whole.at[mine, :],
                    s3.at[self.at, d], r3.at[self.at, d], (in_peers[d], me_out),
                )
                for d in range(1, n_in)
            ]
            sent.extend(self.copies)

        def done(self):
            for c in self.copies:
                c.wait_recv()

    sum_a = Sum(0, 0, half, recv1_a, recv2_a, whole_a)
    sum_b = Sum(1, half, rank, recv1_b, recv2_b, whole_b)
    pl.semaphore_wait(barrier, n_in + n_out - 2)
    sum_a.start()
    sum_b.start()
    sum_a.exchange()
    sum_b.exchange()
    sum_a.gather()
    sum_a.done()

    def flipped(r):
        index = me_in
        for b in range(bits):
            if r >> b & 1:
                bit = lax.rem(me_in // (1 << b), 2)
                index = index + (1 - 2 * bit) * (1 << b)
        return index

    def by_far(count):
        return sorted(range(count), key=lambda r: (-bin(r).count("1"), r))

    peers = [flipped(1 << b) for b in range(bits)]
    order = by_far(n_in // 2)
    up, down = list(range(1, bits)), list(range(bits - 1, 0, -1))
    way = [up if d % 2 else down for d in range(n_out)]
    turns = list(range(1, n_out)) + [0]

    def rows_for(d):
        return pl.ds(pl.multiple_of(out_peers[d] * out_block, out_block), out_block)

    pending = {}
    used = {}

    def landing(h, w, stage, target):
        if stage == rounds - 1:
            return final.at[h, w]
        return stages.at[h, w, (n_in // 2) - (n_in >> (stage + 1)) + target]

    def send_piece(h, w, stage, index, src):
        remaining = sorted(way[w][stage:])
        b = way[w][stage]
        at = remaining.index(b)
        if index >> at & 1:
            target = (index >> (at + 1) << at) | (index & ((1 << at) - 1))
            k = used.get((h, w), 0)
            used[h, w] = k + 1
            copy = remote(
                src, landing(h, w, stage, target), sw.at[h, w, k], rw.at[h, w, k], (peers[b], me_out)
            )
            pending[h, w, stage, target] = copy
            sent.append(copy)

    def product(h, r):
        start = pl.multiple_of(flipped(r) * block, block)
        return dot(basis[h * half : (h + 1) * half, :], ebuf[:, pl.ds(start, block)]).T

    def give(h, r):
        part[h, r] = product(h, 2 * r + 1)
        copy = remote(part.at[h, r], first.at[h, r], sc.at[h, r], rc.at[h, r], (peers[0], me_out))
        pending[h, r] = copy
        sent.append(copy)

    def take(h, r):
        value = product(h, 2 * r)
        pending[h, r].wait_recv()
        first[h, r] = first[h, r] + value
        for w in turns:
            send_piece(h, w, 0, r, first.at[h, r, rows_for(w), :])

    def products(h):
        give(h, order[0])
        for before, r in zip(order, order[1:]):
            give(h, r)
            take(h, before)
        take(h, order[-1])

    def fold(h, stage):
        count = 1 << (len(way[0][stage:]) - 1)
        for target in by_far(count):
            for w in turns:
                at = sorted(way[w][stage:]).index(way[w][stage])
                index = (target >> at << (at + 1)) | (target & ((1 << at) - 1))
                pending[h, w, stage, target].wait_recv()
                if stage == 0:
                    kept = first[h, index, rows_for(w), :]
                else:
                    kept = landing(h, w, stage - 1, index)[...]
                here = landing(h, w, stage, target)
                here[...] = here[...] + kept
                if stage + 1 < rounds:
                    send_piece(h, w, stage + 1, target, here)
                elif w:
                    copy = remote(
                        here, last.at[h, me_out], sz.at[h, w], rz.at[h, w], (me_in, out_peers[w])
                    )
                    pending[h, "z", w] = copy
                    sent.append(copy)
                else:
                    last[h, me_out] = here[...]

    def finish(h):
        for d in range(1, n_out):
            pending[h, "z", d].wait_recv()
        total = last[h, 0]
        for d in range(1, n_out):
            total = total + last[h, d]
        out_ref[:, h * half : (h + 1) * half] = total

    def make_basis(h, left, depth):
        for c in range(0, rows, 512):
            basis[h * half : (h + 1) * half, c : c + 512] = dot(
                left, st[:depth, c : c + 512], HIGHEST
            ).astype(jnp.bfloat16)

    def store_at(at):
        def store(base, value):
            m[at + base : at + base + 8, at : at + half] = value
        return store

    panels = half // 8
    for panel, _ in enumerate(sweep(whole_a[...], store_at(0))):
        if panel == panels // 2:
            sum_b.gather()
    make_basis(0, m[:half, :half], half)
    products(0)
    sum_b.done()
    x = dot(m[:half, :half], whole_b[:, :half].T, HIGHEST)
    y = dot(x.T, m[:half, :half], HIGHEST)
    second = sweep(whole_b[:, half:] - dot(x.T, x, HIGHEST), store_at(half))

    for panel, _ in enumerate(second):
        if panel == panels // 2:
            fold(0, 0)
    m[half:, :half] = -dot(m[half:, half:], y, HIGHEST)
    make_basis(1, m[half:, :], rank)
    for stage in range(1, rounds):
        fold(0, stage)
    products(1)
    for stage in range(rounds):
        fold(1, stage)
    finish(0)
    finish(1)
    for c in sent:
        c.wait_send()


def local(n_in, n_out, embedding, test_matrix):
    rows, width = embedding.shape
    rank = test_matrix.shape[1]
    half = rank // 2
    block = width // n_in
    share = half // n_in
    dma = pltpu.SemaphoreType.DMA
    f32 = jnp.float32
    return pl.pallas_call(
        functools.partial(kernel, n_in, n_out),
        out_shape=jax.ShapeDtypeStruct((block // n_out, rank), f32),
        in_specs=[pl.BlockSpec(memory_space=pl.ANY)] * 2,
        out_specs=pl.BlockSpec(memory_space=pltpu.VMEM),
        scratch_shapes=[
            pltpu.VMEM((rows, width), jnp.bfloat16),
            pltpu.VMEM((width, rank), jnp.bfloat16),
            pltpu.VMEM((rank, 2 * CHUNK), jnp.bfloat16),
            pltpu.VMEM((rank, 2 * CHUNK), jnp.bfloat16),
            pltpu.VMEM((2 * CHUNK, rank), jnp.bfloat16),
            pltpu.VMEM((2 * CHUNK, rank), jnp.bfloat16),
            pltpu.VMEM((rank, rows), f32),
            pltpu.VMEM((rank, rows), jnp.bfloat16),
            pltpu.VMEM((rank, rank), f32),
            pltpu.VMEM((rank, rank), f32),
            pltpu.VMEM((rank, rank), f32),
            pltpu.VMEM((n_in, share, half), f32),
            pltpu.VMEM((n_out, share, half), f32),
            pltpu.VMEM((half, half), f32),
            pltpu.VMEM((n_in, share, rank), f32),
            pltpu.VMEM((n_out, share, rank), f32),
            pltpu.VMEM((half, rank), f32),
            pltpu.VMEM((2, n_in // 2, block, half), f32),
            pltpu.VMEM((2, n_in // 2, block, half), f32),
            pltpu.VMEM((2, n_out, n_in // 2 - 1, block // n_out, half), f32),
            pltpu.VMEM((2, n_out, block // n_out, half), f32),
            pltpu.VMEM((2, n_out, block // n_out, half), f32),
            dma((rows // CHUNK,)), dma,
            dma((2, n_in)), dma((2, n_in)), dma((2, n_out)), dma((2, n_out)), dma((2, n_in)), dma((2, n_in)),
            dma((2, n_in // 2)), dma((2, n_in // 2)),
            dma((2, n_out, n_in // 2)), dma((2, n_out, n_in // 2)),
            dma((2, n_out)), dma((2, n_out)),
        ],
        compiler_params=pltpu.CompilerParams(
            collective_id=0, has_side_effects=True, vmem_limit_bytes=VMEM_LIMIT,
        ),
        cost_estimate=pl.CostEstimate(
            flops=4 * rows * width * rank, bytes_accessed=rows * width * 2, transcendentals=0
        ),
    )(embedding, test_matrix)


def solution(mesh):
    n_in, n_out = mesh.shape["inner"], mesh.shape["outer"]
    return jax.shard_map(
        functools.partial(local, n_in, n_out),
        mesh=mesh,
        in_specs=(P(("inner", "outer"), None), P()),
        out_specs=P(("inner", "outer"), None),
        check_vma=False,
    )
```
